512 devices in a mesh: inst: 64 (over z, x), tp: 8 (over y, core).
Axes of the slice: x: 4, y: 4, z: 16, core: 2. Of those that a mesh axis runs over, the one named last changes fastest.
Arguments:
- cached_state: bfloat16 [128, 8192, 128], P('inst', 'tp'), may hold values from -5 to 5
- kv_pool: bfloat16 [4096, 16, 2048], P('inst', None, 'tp'), may hold values from -5 to 5
- page_table: int32 [128, 32], P('inst'), may hold values from 0 to 63, as said below
- cached_len: int32 [128], replicated, may hold values from 1 to 512
- source_session: int32 [64], replicated, may hold values from 0 to 127, as said below
- turn_len: int32 [64], P('inst'), may hold values from 32 to 128
- x_inner: bfloat16 [8192, 8192], P('inst', 'tp'), may hold values from -80 to 80
- gate_z: bfloat16 [8192, 8192], P('inst', 'tp'), may hold values from -4 to 4
- b_proj: bfloat16 [8192, 1024], P('inst', 'tp'), may hold values from -0.29882812 to 0.29882812
- c_proj: bfloat16 [8192, 1024], P('inst', 'tp'), may hold values from -3 to 3
- step_size: float32 [128, 8192], P('tp', 'inst'), may hold values from 0 to 80, as said below
- decay_rate: float32 [128], P('tp'), may hold values from 0 to 1, as said below
- skip_gain: float32 [128], P('tp'), may hold values from 0.5 to 1.5
- norm_gain: float32 [8192], P('tp'), may hold values from 0.5 to 1.5
- queries: bfloat16 [8192, 8192], P('inst', 'tp'), may hold values from -16 to 16
- new_kv: bfloat16 [8192, 2048], P('inst', 'tp'), may hold values from -5 to 5
Outputs:
- mixer_out: bfloat16 [8192, 8192], P('inst', 'tp')
- attn_out: bfloat16 [8192, 8192], P('inst', 'tp')
- new_state: bfloat16 [64, 8192, 128], P('inst', 'tp')
The draws below stay inside these ranges and needn't reach their ends.
Inputs may be any that keep to these rules, and one draw needn't show every extreme that they name: `page_table`: each instance's 2 x 32 entries are a permutation of its 64 page indices. `source_session`: stored session ids; every instance serves one session, and exactly one of each instance's 2 stored sessions is served. `step_size`: positive. `decay_rate`: positive.
All inputs are finite; a program needn't handle non-finite values.
Results may differ from the reference program's by a relative error of at most 0.0049.
Values may be sent and summed in bfloat16 or wider, within the bound.
A program may use at most 64 MiB of HBM per device.

```python
import math
import jax
import jax.numpy as jnp
from jax import lax

HEADS_DEV = 16
HEAD_DIM = 64
STATE = 128
KV_DIM = 128
QPER = 8
SPAN = 128
PAGE = 16
STORE = 2
REPLY_SLOTS = 128
CACHE = 512
SESSIONS = 64
STORED = 128
HISTORY_SLOTS = 8192
SELECTIVE_SCANS = 128
INNER = 8192
GROUPW = 1024
PAGES = 32
POOL = 64
POOLS = 4096
QWIDTH = 8192
KVW = 2048
N_TP = 8


def served_pick(key):
    order = jax.random.permutation(jax.random.fold_in(key, 101), SESSIONS)
    slots = jax.random.randint(jax.random.fold_in(key, 102), (SESSIONS,), 0, STORE)
    slots = slots.at[0].set(0).at[SESSIONS - 1].set(STORE - 1)
    return (order * STORE + jnp.take(slots, order)).astype(jnp.int32)


def key_base(key):
    return jax.random.normal(jax.random.fold_in(key, 201), (HISTORY_SLOTS, N_TP, KV_DIM), jnp.float32)


def draw_page_table(key, part):
    key = jax.random.fold_in(key, 3)
    holder_keys = jax.random.split(key, SESSIONS)
    orders = jax.vmap(lambda one_key: jax.random.permutation(one_key, POOL))(holder_keys)
    return orders.reshape(STORED, PAGES).astype(jnp.int32)


def draw_cached_len(key, part):
    served = served_pick(key)
    key = jax.random.fold_in(key, 2)
    lengths = jax.random.randint(jax.random.fold_in(key, 1), (STORED,), 1, CACHE + 1)
    longest = jax.random.randint(jax.random.fold_in(key, 2), (), 0, SESSIONS)
    shortest = (longest + 1 + jax.random.randint(jax.random.fold_in(key, 3), (), 0, SESSIONS - 1)) % SESSIONS
    lengths = lengths.at[jnp.take(served, longest)].set(CACHE)
    lengths = lengths.at[jnp.take(served, shortest)].set(1)
    return lengths.astype(jnp.int32)


def draw_source_session(key, part):
    served = served_pick(key)
    return served


def draw_turn_len(key, part):
    key = jax.random.fold_in(key, 9)
    lengths = jax.random.randint(jax.random.fold_in(key, 1), (SESSIONS,), REPLY_SLOTS // 4, REPLY_SLOTS + 1)
    longest = jax.random.randint(jax.random.fold_in(key, 2), (), 0, SESSIONS)
    shortest = (longest + 1 + jax.random.randint(jax.random.fold_in(key, 3), (), 0, SESSIONS - 1)) % SESSIONS
    lengths = lengths.at[longest].set(REPLY_SLOTS)
    lengths = lengths.at[shortest].set(REPLY_SLOTS // 4)
    return lengths.astype(jnp.int32)


def draw_x_inner(key, part):
    key = jax.random.fold_in(key, 6)
    first_key, latter_random_start, third_key = jax.random.split(key, 3)
    column = jnp.arange(INNER, dtype=jnp.float32) / (INNER - 1)
    column_scale = 10.0 ** (jax.random.uniform(latter_random_start, (INNER,)) - 0.5)
    row_scale = 10.0 ** (jax.random.uniform(third_key, (HISTORY_SLOTS,)) - 0.5)
    starting_shift = jnp.clip(jax.random.normal(first_key, (HISTORY_SLOTS, INNER)), -4.0, 4.0)
    ramp = 3.0 ** (column - 0.5)
    return (starting_shift * (column_scale * ramp)[None, :] * row_scale[:, None]).astype(jnp.bfloat16)


def draw_step_size(key, part):
    key = jax.random.fold_in(key, 4)
    first_key, latter_random_start, third_key = jax.random.split(key, 3)
    starting_shift = jax.nn.softplus(0.5 * jax.random.normal(first_key, (SELECTIVE_SCANS, HISTORY_SLOTS)) - 0.6)
    spurt_extent = jax.random.randint(latter_random_start, (SELECTIVE_SCANS, HISTORY_SLOTS), 0, REPLY_SLOTS) < 3
    vertical_number = jax.random.uniform(third_key, (SELECTIVE_SCANS, HISTORY_SLOTS), minval=20.0, maxval=60.0)
    return jnp.where(spurt_extent, vertical_number, starting_shift)


def draw_decay_rate(key, part):
    key = jax.random.fold_in(key, 5)
    lowest = math.log(0.5 / REPLY_SLOTS)
    highest = math.log(0.06)
    spread = jax.random.uniform(key, (SELECTIVE_SCANS,))
    return jnp.exp(lowest + spread * (highest - lowest))


def draw_new_kv(key, part):
    starting_shift = key_base(key)
    key = jax.random.fold_in(key, 7)
    key_part = jnp.clip(starting_shift, -5.0, 5.0)
    value_part = jnp.clip(jax.random.normal(key, (HISTORY_SLOTS, N_TP, KV_DIM)), -5.0, 5.0)
    return jnp.stack([key_part, value_part], axis=2).reshape(HISTORY_SLOTS, KVW).astype(jnp.bfloat16)


def draw_queries(key, part):
    key = jax.random.fold_in(key, 8)
    query_part = jnp.clip(jax.random.normal(key, (HISTORY_SLOTS, N_TP, QPER, KV_DIM)), -5.0, 5.0)
    return query_part.reshape(HISTORY_SLOTS, QWIDTH).astype(jnp.bfloat16)


def levels(key, extent, shards, smallest, top_value):
    loudness, own = 1.0, jax.random.fold_in(key, 6)
    for dim, blocks in shards:
        heights = jnp.exp(jax.random.uniform(jax.random.fold_in(own, dim), (blocks,), jnp.float32, smallest / len(shards), top_value / len(shards)))
        loudness = loudness * jnp.repeat(heights, extent[dim] // blocks).reshape([-1 if axis == dim else 1 for axis in range(len(extent))])
    return loudness


def normal_values(stream_key, shape, width, bound, cuts=(), held_as=jnp.bfloat16):
    factor_of = levels(stream_key, shape, cuts, -0.22, 0.18) if cuts else 1.0
    values = jax.random.normal(stream_key, shape, jnp.float32) * width * factor_of
    return jnp.minimum(jnp.maximum(values, -bound), bound).astype(held_as)


def setup_inputs(seed: int = 0) -> dict:
    splits = jax.random.split(jax.random.key(seed), 17)
    return {
        "cached_state": normal_values(splits[0], (STORED, INNER, STATE), 1.0, 5.0, ((0, 64), (1, 8))),
        "kv_pool": normal_values(splits[1], (POOLS, PAGE, KVW), 1.0, 5.0, ((0, 64), (2, 8))),
        "page_table": draw_page_table(jax.random.fold_in(splits[16], 71), 0),
        "cached_len": draw_cached_len(jax.random.fold_in(splits[16], 71), 0),
        "source_session": draw_source_session(jax.random.fold_in(splits[16], 71), 0),
        "turn_len": draw_turn_len(jax.random.fold_in(splits[16], 71), 0),
        "x_inner": draw_x_inner(jax.random.fold_in(splits[16], 71), 0),
        "gate_z": normal_values(splits[7], (HISTORY_SLOTS, INNER), 1.0, 4.0, ((0, 64), (1, 8))),
        "b_proj": normal_values(splits[8], (HISTORY_SLOTS, GROUPW), 0.05, 0.29882812, ((0, 64), (1, 8))),
        "c_proj": normal_values(splits[9], (HISTORY_SLOTS, GROUPW), 0.5, 3.0, ((0, 64), (1, 8))),
        "step_size": draw_step_size(jax.random.fold_in(splits[16], 71), 0),
        "decay_rate": draw_decay_rate(jax.random.fold_in(splits[16], 71), 0),
        "skip_gain": jnp.clip(0.5 + 1.0 * jax.random.uniform(splits[12], (SELECTIVE_SCANS,), jnp.float32) ** levels(splits[12], (SELECTIVE_SCANS,), ((0, 8),), -0.2, 0.2), 0.5, 1.5),
        "norm_gain": jnp.clip(1.0 + 0.1 * jax.random.normal(splits[13], (INNER,), jnp.float32), 0.5, 1.5),
        "queries": draw_queries(jax.random.fold_in(splits[16], 71), 0),
        "new_kv": draw_new_kv(jax.random.fold_in(splits[16], 71), 0),
    }


exact_mode = lax.Precision.HIGHEST
EPSILON = 1e-05

def mixer_session(x_rows, z_rows, b_rows, c_rows, dt_rows, decay_rate, skip_gain, norm_gain, start_state, length):
    positions = jnp.arange(REPLY_SLOTS, dtype=jnp.int32)
    live_rows = positions < length
    dt_live = jnp.where(live_rows[None, :], dt_rows, jnp.float32(0.0))
    log_decay = -dt_live * decay_rate[:, None]
    x_heads = x_rows.reshape(REPLY_SLOTS, SELECTIVE_SCANS, HEAD_DIM).astype(jnp.float32)
    b_heads = jnp.repeat(b_rows.reshape(REPLY_SLOTS, N_TP, STATE), HEADS_DEV, axis=1).astype(jnp.float32)
    c_heads = jnp.repeat(c_rows.reshape(REPLY_SLOTS, N_TP, STATE), HEADS_DEV, axis=1).astype(jnp.float32)
    lower_mask = positions[:SPAN, None] >= positions[None, :SPAN]
    state_now = start_state
    outputs = []
    for block_index in range(REPLY_SLOTS // SPAN):
        first = block_index * SPAN
        x_block = x_heads[first:first + SPAN]
        b_block = b_heads[first:first + SPAN]
        c_block = c_heads[first:first + SPAN]
        dt_block = dt_live[:, first:first + SPAN]
        cumulative = jnp.cumsum(log_decay[:, first:first + SPAN], axis=1)
        differ = cumulative[:, :, None] - cumulative[:, None, :]
        decay_table = jnp.where(lower_mask[None], jnp.exp(jnp.where(lower_mask[None], differ, 0.0)), 0.0)
        products = jnp.einsum('ihn,jhn->hij', c_block, b_block)
        weights = lax.optimization_barrier((products * decay_table * dt_block[:, None, :]).astype(jnp.bfloat16)).astype(jnp.float32)
        intra = jnp.einsum('hij,jhp->ihp', weights, x_block)
        carried = jnp.einsum('hpn,ihn->ihp', state_now, c_block, precision=exact_mode)
        inter = jnp.exp(cumulative).T[:, :, None] * carried
        final_log = cumulative[:, -1]
        tail_weight = jnp.exp(final_log[:, None] - cumulative) * dt_block
        mixed_b = lax.optimization_barrier((tail_weight.T[:, :, None] * b_block).astype(jnp.bfloat16)).astype(jnp.float32)
        fresh_state = jnp.einsum('jhp,jhn->hpn', x_block, mixed_b)
        state_now = jnp.exp(final_log)[:, None, None] * state_now + fresh_state
        outputs.append(intra + inter + skip_gain[None, :, None] * x_block)
    raw_rows = jnp.concatenate(outputs, axis=0).reshape(REPLY_SLOTS, INNER)
    gated = raw_rows * jax.nn.silu(z_rows.astype(jnp.float32))
    mean_square = lax.optimization_barrier(jnp.sum(gated * gated, axis=1)) / INNER
    normed = gated * lax.rsqrt(mean_square + EPSILON)[:, None] * norm_gain[None, :]
    mixer_rows = jnp.where(live_rows[:, None], normed, 0.0).astype(jnp.bfloat16)
    return (mixer_rows, state_now.reshape(INNER, STATE).astype(jnp.bfloat16))

def attention_session(query_rows, new_rows, cache_rows, cached_count, length):
    score_scale = KV_DIM ** (-0.5)
    query_heads = query_rows.reshape(REPLY_SLOTS, N_TP, QPER, KV_DIM).astype(jnp.float32)
    cache_split = cache_rows.reshape(CACHE, N_TP, 2, KV_DIM)
    new_split = new_rows.reshape(REPLY_SLOTS, N_TP, 2, KV_DIM)
    all_keys = jnp.concatenate([cache_split[:, :, 0], new_split[:, :, 0]], axis=0).astype(jnp.float32)
    all_values = jnp.concatenate([cache_split[:, :, 1], new_split[:, :, 1]], axis=0).astype(jnp.float32)
    scores = jnp.einsum('tgqd,kgd->gqtk', query_heads, all_keys) * score_scale
    key_index = jnp.arange(CACHE + REPLY_SLOTS, dtype=jnp.int32)
    row_index = jnp.arange(REPLY_SLOTS, dtype=jnp.int32)
    visible = jnp.where(key_index[None, :] < CACHE, key_index[None, :] < cached_count, key_index[None, :] - CACHE <= row_index[:, None])
    masked = jnp.where(visible, scores, -jnp.inf)
    row_max = lax.optimization_barrier(jnp.max(masked, axis=3, keepdims=True))
    raised = jnp.where(visible, jnp.exp(masked - row_max), 0.0)
    probs = lax.optimization_barrier((raised / lax.optimization_barrier(jnp.sum(raised, axis=3, keepdims=True))).astype(jnp.bfloat16)).astype(jnp.float32)
    mixed = jnp.einsum('gqtk,kgd->tgqd', probs, all_values).reshape(REPLY_SLOTS, QWIDTH)
    live_rows = row_index < length
    return jnp.where(live_rows[:, None], mixed, 0.0).astype(jnp.bfloat16)

def reference(cached_state, kv_pool, page_table, cached_len, source_session, turn_len, x_inner, gate_z, b_proj, c_proj, step_size, decay_rate, skip_gain, norm_gain, queries, new_kv):

    def serve(session):
        stored_id = source_session[session]
        holder = stored_id // STORE
        start_state = cached_state[stored_id].astype(jnp.float32).reshape(SELECTIVE_SCANS, HEAD_DIM, STATE)
        page_rows = (holder * POOL + page_table[stored_id]).astype(jnp.int32)
        cache_rows = jnp.take(kv_pool, page_rows, axis=0).reshape(CACHE, KVW)
        first = (session * REPLY_SLOTS).astype(jnp.int32)

        def rows_of(array):
            return lax.dynamic_slice_in_dim(array, first, REPLY_SLOTS, 0)
        dt_rows = lax.dynamic_slice_in_dim(step_size, first, REPLY_SLOTS, 1)
        mixer_rows, state_rows = mixer_session(rows_of(x_inner), rows_of(gate_z), rows_of(b_proj), rows_of(c_proj), dt_rows, decay_rate, skip_gain, norm_gain, start_state, turn_len[session])
        attn_rows = attention_session(rows_of(queries), rows_of(new_kv), cache_rows, cached_len[stored_id], turn_len[session])
        return (mixer_rows, attn_rows, state_rows)
    mixer_all, attn_all, state_all = lax.map(serve, jnp.arange(SESSIONS, dtype=jnp.int32))
    return (mixer_all.reshape(HISTORY_SLOTS, INNER), attn_all.reshape(HISTORY_SLOTS, QWIDTH), state_all)
```

```python
import functools

import jax
import jax.numpy as jnp
from jax import lax
from jax.experimental import pallas as pl
from jax.experimental.pallas import tpu as pltpu
from jax.sharding import PartitionSpec as P

MESH = pl.DeviceIdType.MESH
HEAD_DIM = 64
LANES = 128
PAGE = 16
EPSILON = 1e-05
SCORE_SCALE = 128 ** (-0.5)
FAR_BELOW = -1e30


def serve_kernel(
    instances,
    ranks,
    source_ref,
    cached_len_ref,
    page_ref,
    turn_len_ref,
    rate_ref,
    skip_ref,
    state_ref,
    kv_ref,
    x_ref,
    z_ref,
    b_ref,
    c_ref,
    dt_ref,
    gain_ref,
    q_ref,
    new_ref,
    mixer_ref,
    attn_ref,
    new_state_ref,
    state_out,
    state_mid,
    state_fwd,
    state_in,
    kv_out,
    kv_mid,
    kv_fwd,
    kv_in,
    square_out,
    square_in,
    raw,
    reach,
    silu,
    fresh,
    send_sem,
    recv_sem,
    square_send,
    square_recv,
):
    me = lax.axis_index("inst")
    rank = lax.axis_index("tp")
    others = instances - 1
    barrier = pltpu.get_barrier_semaphore()

    def greet(k, carry):
        peer = lax.rem(me + k, instances)
        pl.semaphore_signal(barrier, inc=1, device_id={"inst": peer}, device_id_type=MESH)
        return carry

    lax.fori_loop(1, instances, greet, 0)

    def greet_rank(k, carry):
        peer = lax.rem(rank + k, ranks)
        pl.semaphore_signal(barrier, inc=1, device_id={"tp": peer}, device_id_type=MESH)
        return carry

    lax.fori_loop(1, ranks, greet_rank, 0)

    def find(d, found):
        g = source_ref[d]
        return found + jnp.where(lax.shift_right_logical(g, 1) == me, g & 1, 0)

    slot = lax.fori_loop(0, instances, find, jnp.int32(0))
    state_out[...] = state_ref[slot]
    for page in range(instances // 2):
        rows = kv_ref[page_ref[slot, page]]
        kv_out[2 * page] = rows[:, :LANES]
        kv_out[2 * page + 1] = rows[:, LANES:]

    pl.semaphore_wait(barrier, others + ranks - 1)

    def partner(k):
        step = (k + 2) // 2
        return lax.rem(me + instances + step * (1 - 2 * (k % 2)), instances)

    def spread(out, mid, phase):
        def send(k, carry):
            peer = partner(k)
            pltpu.make_async_remote_copy(
                src_ref=out.at[peer],
                dst_ref=mid.at[me],
                send_sem=send_sem.at[phase],
                recv_sem=recv_sem.at[phase],
                device_id={"inst": peer},
                device_id_type=MESH,
            ).start()
            return carry

        lax.fori_loop(0, others, send, 0)
        mid[me] = out[me]

    def collect(mid, fwd, arrive, phase):
        def send(k, carry):
            peer = partner(k)
            holder = lax.shift_right_logical(source_ref[peer], 1)
            fwd[peer] = mid[holder]
            pltpu.make_async_remote_copy(
                src_ref=fwd.at[peer],
                dst_ref=arrive.at[me],
                send_sem=send_sem.at[phase],
                recv_sem=recv_sem.at[phase],
                device_id={"inst": peer},
                device_id_type=MESH,
            ).start()
            return carry

        lax.fori_loop(0, others, send, 0)
        arrive[me] = mid[lax.shift_right_logical(source_ref[me], 1)]

    def arrived(buffer, phase):
        part = buffer.at[pl.ds(0, others)]
        pltpu.make_async_copy(part, part, recv_sem.at[phase]).wait()

    def sent(buffer, phase):
        part = buffer.at[pl.ds(0, others)]
        pltpu.make_async_copy(part, part, send_sem.at[phase]).wait()

    spread(state_out, state_mid, 0)
    spread(kv_out, kv_mid, 1)

    length = turn_len_ref[0]
    tokens = x_ref.shape[0]
    heads = dt_ref.shape[0]
    tiles = x_ref.shape[1] // LANES
    row_id = lax.broadcasted_iota(jnp.int32, (tokens, tokens), 0)
    col_id = lax.broadcasted_iota(jnp.int32, (tokens, tokens), 1)
    lower = row_id >= col_id
    first_head = col_id < HEAD_DIM
    head_id = lax.broadcasted_iota(jnp.int32, (heads, tokens), 0)
    token_id = lax.broadcasted_iota(jnp.int32, (heads, tokens), 1)
    rate = jnp.zeros((heads, tokens), jnp.float32)
    for h in range(heads):
        rate = jnp.where(head_id == h, rate_ref[h], rate)
    dt = jnp.where(token_id < length, dt_ref[...], 0.0)
    log_decay = -dt * rate
    cumulative = lax.dot_general(
        log_decay,
        lower.astype(jnp.float32),
        (((1,), (1,)), ((), ())),
        precision=lax.Precision.HIGHEST,
        preferred_element_type=jnp.float32,
    )
    last = jnp.broadcast_to(cumulative[:, tokens - 1 : tokens], (heads, tokens))
    tail = jnp.exp(last - cumulative) * dt
    final = jnp.exp(last)
    stacked = jnp.concatenate(
        [
            cumulative,
            jnp.exp(cumulative),
            tail,
            jnp.zeros((tokens - 3 * heads, tokens), jnp.float32),
        ],
        axis=0,
    )
    columns = jnp.transpose(stacked)

    def column(index):
        return jnp.broadcast_to(columns[:, index : index + 1], (tokens, tokens))

    b = b_ref[...]
    c = c_ref[...]
    b_wide = b.astype(jnp.float32)
    products = lax.dot_general(
        c, b, (((1,), (1,)), ((), ())), preferred_element_type=jnp.float32
    )
    for pair in range(tiles):
        span = slice(pair * LANES, (pair + 1) * LANES)
        x = x_ref[:, span]
        parts = []
        mixed = []
        for h in (2 * pair, 2 * pair + 1):
            differ = column(h) - cumulative[h : h + 1, :]
            decay = jnp.exp(jnp.where(lower, differ, FAR_BELOW))
            weights = (products * decay * dt[h : h + 1, :]).astype(jnp.bfloat16)
            parts.append(jnp.dot(weights, x, preferred_element_type=jnp.float32))
            mixed.append((column(2 * heads + h) * b_wide).astype(jnp.bfloat16))
        gain = jnp.where(first_head, skip_ref[2 * pair], skip_ref[2 * pair + 1])
        raw[:, span] = jnp.where(first_head, parts[0], parts[1]) + gain * x.astype(
            jnp.float32
        )
        reach[:, span] = jnp.where(
            first_head, column(heads + 2 * pair), column(heads + 2 * pair + 1)
        )
        z = z_ref[:, span].astype(jnp.float32)
        silu[:, span] = z / (1.0 + jnp.exp(-z))
        both = lax.dot_general(
            x,
            jnp.concatenate(mixed, axis=1),
            (((0,), (0,)), ((), ())),
            preferred_element_type=jnp.float32,
        )
        top = pair * LANES
        fresh[top : top + HEAD_DIM] = both[:HEAD_DIM, :LANES]
        fresh[top + HEAD_DIM : top + LANES] = both[HEAD_DIM:, LANES:]

    arrived(state_mid, 0)
    collect(state_mid, state_fwd, state_in, 2)
    arrived(kv_mid, 1)
    collect(kv_mid, kv_fwd, kv_in, 3)

    arrived(state_in, 2)
    state = state_in[...].reshape(x_ref.shape[1], LANES)
    total = jnp.zeros((tokens, LANES), jnp.float32)
    for pair in range(tiles):
        span = slice(pair * LANES, (pair + 1) * LANES)
        carried = lax.dot_general(
            c, state[span], (((1,), (1,)), ((), ())), preferred_element_type=jnp.float32
        )
        gated = (raw[:, span] + reach[:, span] * carried) * silu[:, span]
        raw[:, span] = gated
        total = total + gated * gated
    squares = jnp.sum(jnp.transpose(total), axis=0, keepdims=True)
    square_out[...] = jnp.broadcast_to(squares, square_out.shape)
    square_in[rank] = jnp.broadcast_to(squares, square_out.shape)

    def tell(k, carry):
        peer = lax.rem(rank + k, ranks)
        pltpu.make_async_remote_copy(
            src_ref=square_out,
            dst_ref=square_in.at[rank],
            send_sem=square_send,
            recv_sem=square_recv,
            device_id={"tp": peer},
            device_id_type=MESH,
        ).start()
        return carry

    lax.fori_loop(1, ranks, tell, 0)
    for h in range(heads):
        span = slice(h * HEAD_DIM, (h + 1) * HEAD_DIM)
        new_state_ref[span] = (
            final[h : h + 1, :] * state[span].astype(jnp.float32) + fresh[span]
        ).astype(jnp.bfloat16)

    part = square_in.at[pl.ds(0, ranks - 1)]
    pltpu.make_async_copy(part, part, square_recv).wait()
    mean = jnp.sum(square_in[...], axis=0) / (x_ref.shape[1] * ranks)
    scale = lax.rsqrt(mean + EPSILON)
    scale = jnp.transpose(jnp.broadcast_to(scale[:1], (tokens, tokens)))
    live = row_id < length
    scale = jnp.where(live, scale, 0.0)
    for pair in range(tiles):
        span = slice(pair * LANES, (pair + 1) * LANES)
        mixer_ref[:, span] = (raw[:, span] * scale * gain_ref[:, span]).astype(jnp.bfloat16)

    cached = cached_len_ref[source_ref[me]]
    keys_new = new_ref[:, :LANES]
    values_new = new_ref[:, LANES:]
    arrived(kv_in, 3)
    keys = []
    values = []
    for page in range(instances // 2):
        keys.append(kv_in[2 * page])
        values.append(kv_in[2 * page + 1])
    keys = jnp.concatenate(keys, axis=0)
    values = jnp.concatenate(values, axis=0)
    cache_rows = keys.shape[0]
    key_id = lax.broadcasted_iota(jnp.int32, (tokens, cache_rows), 1)
    seen = key_id < cached
    for head in range(tiles):
        span = slice(head * LANES, (head + 1) * LANES)
        query = q_ref[:, span]
        old = lax.dot_general(
            query, keys, (((1,), (1,)), ((), ())), preferred_element_type=jnp.float32
        )
        new = lax.dot_general(
            query, keys_new, (((1,), (1,)), ((), ())), preferred_element_type=jnp.float32
        )
        old = jnp.where(seen, old, FAR_BELOW)
        new = jnp.where(lower, new, FAR_BELOW)
        top = jnp.maximum(
            jnp.max(old, axis=1, keepdims=True), jnp.max(new, axis=1, keepdims=True)
        )
        old = jnp.exp((old - top) * SCORE_SCALE)
        new = jnp.exp((new - top) * SCORE_SCALE)
        weight = jnp.sum(old, axis=1, keepdims=True) + jnp.sum(new, axis=1, keepdims=True)
        out = jnp.dot(
            old.astype(jnp.bfloat16), values, preferred_element_type=jnp.float32
        ) + jnp.dot(new.astype(jnp.bfloat16), values_new, preferred_element_type=jnp.float32)
        attn_ref[:, span] = jnp.where(live, out / weight, 0.0).astype(jnp.bfloat16)

    sent(state_out, 0)
    sent(kv_out, 1)
    sent(state_fwd, 2)
    sent(kv_fwd, 3)
    part = square_in.at[pl.ds(0, ranks - 1)]
    pltpu.make_async_copy(part, part, square_send).wait()


def on_device(
    instances,
    ranks,
    cached_state,
    kv_pool,
    page_table,
    cached_len,
    source_session,
    turn_len,
    x_inner,
    gate_z,
    b_proj,
    c_proj,
    step_size,
    decay_rate,
    skip_gain,
    norm_gain,
    queries,
    new_kv,
):
    stores, rows, width = cached_state.shape
    piece = (instances, PAGE, LANES)
    tokens, inner = x_inner.shape
    smem = pl.BlockSpec(memory_space=pltpu.SMEM)
    vmem = pl.BlockSpec(memory_space=pltpu.VMEM)
    mixer_out, attn_out, new_state = pl.pallas_call(
        functools.partial(serve_kernel, instances, ranks),
        out_shape=(
            jax.ShapeDtypeStruct((tokens, inner), jnp.bfloat16),
            jax.ShapeDtypeStruct((tokens, inner), jnp.bfloat16),
            jax.ShapeDtypeStruct((rows, width), jnp.bfloat16),
        ),
        in_specs=[smem] * 6 + [vmem] * 10,
        out_specs=(vmem,) * 3,
        scratch_shapes=[pltpu.VMEM(piece, jnp.bfloat16)] * 8
        + [
            pltpu.VMEM((8, LANES), jnp.float32),
            pltpu.VMEM((ranks, 8, LANES), jnp.float32),
            pltpu.VMEM((tokens, inner), jnp.float32),
            pltpu.VMEM((tokens, inner), jnp.float32),
            pltpu.VMEM((tokens, inner), jnp.float32),
            pltpu.VMEM((rows, width), jnp.float32),
            pltpu.SemaphoreType.DMA((4,)),
            pltpu.SemaphoreType.DMA((4,)),
            pltpu.SemaphoreType.DMA,
            pltpu.SemaphoreType.DMA,
        ],
        compiler_params=pltpu.CompilerParams(
            collective_id=0, has_side_effects=True, vmem_limit_bytes=48 * 1024 * 1024
        ),
    )(
        source_session,
        cached_len,
        page_table,
        turn_len,
        decay_rate,
        skip_gain,
        cached_state.reshape(stores, instances, PAGE, width),
        kv_pool,
        x_inner,
        gate_z,
        b_proj,
        c_proj,
        step_size,
        norm_gain.reshape(1, inner),
        queries,
        new_kv,
    )
    return (mixer_out, attn_out, new_state.reshape(1, rows, width))


def solution(mesh):
    in_specs = (
        P("inst", "tp", None),
        P("inst", None, "tp"),
        P("inst", None),
        P(),
        P(),
        P("inst"),
        P("inst", "tp"),
        P("inst", "tp"),
        P("inst", "tp"),
        P("inst", "tp"),
        P("tp", "inst"),
        P("tp"),
        P("tp"),
        P("tp"),
        P("inst", "tp"),
        P("inst", "tp"),
    )
    out_specs = (P("inst", "tp"), P("inst", "tp"), P("inst", "tp", None))
    body = functools.partial(on_device, mesh.shape["inst"], mesh.shape["tp"])
    return jax.shard_map(
        body, mesh=mesh, in_specs=in_specs, out_specs=out_specs, check_vma=False
    )
```

```python
import functools

import jax
import jax.numpy as jnp
from jax import lax
from jax.experimental import pallas as pl
from jax.experimental.pallas import tpu as pltpu
from jax.sharding import PartitionSpec as P

MESH = pl.DeviceIdType.MESH
HEAD_DIM = 64
LANES = 128
PAGE = 16
EPSILON = 1e-05
SCORE_SCALE = 128 ** (-0.5)
FAR_BELOW = -1e30
N_OPERANDS = 16
N_OUTPUTS = 3


def serve_kernel(
    instances,
    ranks,
    *refs,
):
    operands, refs = refs[:N_OPERANDS], refs[N_OPERANDS:]
    outputs, refs = refs[:N_OUTPUTS], refs[N_OUTPUTS:]
    held, refs = refs[:N_OPERANDS], refs[N_OPERANDS:]
    results, refs = refs[:N_OUTPUTS], refs[N_OUTPUTS:]
    (
        source_ref,
        page_ref,
        state_ref,
        kv_ref,
        turn_len_ref,
        rate_ref,
        skip_ref,
        x_ref,
        b_ref,
        c_ref,
        dt_ref,
        z_ref,
        gain_ref,
        cached_len_ref,
        q_ref,
        new_ref,
    ) = held
    mixer_ref, attn_ref, new_state_ref = results
    (
    state_out,
    state_mid,
    state_fwd,
    state_in,
    kv_out,
    kv_mid,
    kv_fwd,
    kv_in,
    square_out,
    square_in,
    raw,
    reach,
    silu,
    fresh,
    send_sem,
    recv_sem,
    square_send,
    square_recv,
    fetch_sem,
    store_sem,
    ) = refs
    me = lax.axis_index("inst")
    rank = lax.axis_index("tp")
    others = instances - 1
    barrier = pltpu.get_barrier_semaphore()
    fetches = [
        pltpu.make_async_copy(operands[i], held[i], fetch_sem.at[i])
        for i in range(N_OPERANDS)
    ]
    stores = [
        pltpu.make_async_copy(results[i], outputs[i], store_sem.at[i])
        for i in range(N_OUTPUTS)
    ]
    for fetch in fetches[:4]:
        fetch.start()

    def greet(k, carry):
        peer = lax.rem(me + k, instances)
        pl.semaphore_signal(barrier, inc=1, device_id={"inst": peer}, device_id_type=MESH)
        return carry

    lax.fori_loop(1, instances, greet, 0)

    def greet_rank(k, carry):
        peer = lax.rem(rank + k, ranks)
        pl.semaphore_signal(barrier, inc=1, device_id={"tp": peer}, device_id_type=MESH)
        return carry

    lax.fori_loop(1, ranks, greet_rank, 0)

    for fetch in fetches[4:]:
        fetch.start()
    fetches[0].wait()

    def find(d, found):
        g = source_ref[d]
        return found + jnp.where(lax.shift_right_logical(g, 1) == me, g & 1, 0)

    slot = lax.fori_loop(0, instances, find, jnp.int32(0))
    fetches[1].wait()
    fetches[2].wait()
    state_out[...] = state_ref[slot]
    fetches[3].wait()
    for page in range(instances // 2):
        rows = kv_ref[page_ref[slot, page]]
        kv_out[2 * page] = rows[:, :LANES]
        kv_out[2 * page + 1] = rows[:, LANES:]

    pl.semaphore_wait(barrier, others + ranks - 1)

    def partner(k):
        step = (k + 2) // 2
        return lax.rem(me + instances + step * (1 - 2 * (k % 2)), instances)

    def spread(out, mid, phase):
        def send(k, carry):
            peer = partner(k)
            pltpu.make_async_remote_copy(
                src_ref=out.at[peer],
                dst_ref=mid.at[me],
                send_sem=send_sem.at[phase],
                recv_sem=recv_sem.at[phase],
                device_id={"inst": peer},
                device_id_type=MESH,
            ).start()
            return carry

        lax.fori_loop(0, others, send, 0)
        mid[me] = out[me]

    def collect(mid, fwd, arrive, phase):
        def send(k, carry):
            peer = partner(k)
            holder = lax.shift_right_logical(source_ref[peer], 1)
            fwd[peer] = mid[holder]
            pltpu.make_async_remote_copy(
                src_ref=fwd.at[peer],
                dst_ref=arrive.at[me],
                send_sem=send_sem.at[phase],
                recv_sem=recv_sem.at[phase],
                device_id={"inst": peer},
                device_id_type=MESH,
            ).start()
            return carry

        lax.fori_loop(0, others, send, 0)
        arrive[me] = mid[lax.shift_right_logical(source_ref[me], 1)]

    def arrived(buffer, phase):
        part = buffer.at[pl.ds(0, others)]
        pltpu.make_async_copy(part, part, recv_sem.at[phase]).wait()

    def sent(buffer, phase):
        part = buffer.at[pl.ds(0, others)]
        pltpu.make_async_copy(part, part, send_sem.at[phase]).wait()

    spread(state_out, state_mid, 0)
    spread(kv_out, kv_mid, 1)

    for fetch in fetches[4:]:
        fetch.wait()
    length = turn_len_ref[0]
    tokens = x_ref.shape[0]
    heads = dt_ref.shape[0]
    tiles = x_ref.shape[1] // LANES
    row_id = lax.broadcasted_iota(jnp.int32, (tokens, tokens), 0)
    col_id = lax.broadcasted_iota(jnp.int32, (tokens, tokens), 1)
    lower = row_id >= col_id
    first_head = col_id < HEAD_DIM
    head_id = lax.broadcasted_iota(jnp.int32, (heads, tokens), 0)
    token_id = lax.broadcasted_iota(jnp.int32, (heads, tokens), 1)
    rate = jnp.zeros((heads, tokens), jnp.float32)
    for h in range(heads):
        rate = jnp.where(head_id == h, rate_ref[h], rate)
    dt = jnp.where(token_id < length, dt_ref[...], 0.0)
    log_decay = -dt * rate
    cumulative = lax.dot_general(
        log_decay,
        lower.astype(jnp.float32),
        (((1,), (1,)), ((), ())),
        precision=lax.Precision.HIGHEST,
        preferred_element_type=jnp.float32,
    )
    last = jnp.broadcast_to(cumulative[:, tokens - 1 : tokens], (heads, tokens))
    tail = jnp.exp(last - cumulative) * dt
    final = jnp.exp(last)
    stacked = jnp.concatenate(
        [
            cumulative,
            jnp.exp(cumulative),
            tail,
            jnp.zeros((tokens - 3 * heads, tokens), jnp.float32),
        ],
        axis=0,
    )
    columns = jnp.transpose(stacked)

    def column(index):
        return jnp.broadcast_to(columns[:, index : index + 1], (tokens, tokens))

    b = b_ref[...]
    c = c_ref[...]
    b_wide = b.astype(jnp.float32)
    products = lax.dot_general(
        c, b, (((1,), (1,)), ((), ())), preferred_element_type=jnp.float32
    )
    for pair in range(tiles):
        span = slice(pair * LANES, (pair + 1) * LANES)
        x = x_ref[:, span]
        parts = []
        mixed = []
        for h in (2 * pair, 2 * pair + 1):
            differ = column(h) - cumulative[h : h + 1, :]
            decay = jnp.exp(jnp.where(lower, differ, FAR_BELOW))
            weights = (products * decay * dt[h : h + 1, :]).astype(jnp.bfloat16)
            parts.append(jnp.dot(weights, x, preferred_element_type=jnp.float32))
            mixed.append((column(2 * heads + h) * b_wide).astype(jnp.bfloat16))
        gain = jnp.where(first_head, skip_ref[2 * pair], skip_ref[2 * pair + 1])
        raw[:, span] = jnp.where(first_head, parts[0], parts[1]) + gain * x.astype(
            jnp.float32
        )
        reach[:, span] = jnp.where(
            first_head, column(heads + 2 * pair), column(heads + 2 * pair + 1)
        )
        z = z_ref[:, span].astype(jnp.float32)
        silu[:, span] = z / (1.0 + jnp.exp(-z))
        both = lax.dot_general(
            x,
            jnp.concatenate(mixed, axis=1),
            (((0,), (0,)), ((), ())),
            preferred_element_type=jnp.float32,
        )
        top = pair * LANES
        fresh[top : top + HEAD_DIM] = both[:HEAD_DIM, :LANES]
        fresh[top + HEAD_DIM : top + LANES] = both[HEAD_DIM:, LANES:]

    arrived(state_mid, 0)
    collect(state_mid, state_fwd, state_in, 2)
    arrived(kv_mid, 1)
    collect(kv_mid, kv_fwd, kv_in, 3)

    arrived(state_in, 2)
    state = state_in[...].reshape(x_ref.shape[1], LANES)
    total = jnp.zeros((tokens, LANES), jnp.float32)
    for pair in range(tiles):
        span = slice(pair * LANES, (pair + 1) * LANES)
        carried = lax.dot_general(
            c, state[span], (((1,), (1,)), ((), ())), preferred_element_type=jnp.float32
        )
        gated = (raw[:, span] + reach[:, span] * carried) * silu[:, span]
        raw[:, span] = gated
        total = total + gated * gated
    squares = jnp.sum(jnp.transpose(total), axis=0, keepdims=True)
    square_out[...] = jnp.broadcast_to(squares, square_out.shape)
    square_in[rank] = jnp.broadcast_to(squares, square_out.shape)

    def tell(k, carry):
        peer = lax.rem(rank + k, ranks)
        pltpu.make_async_remote_copy(
            src_ref=square_out,
            dst_ref=square_in.at[rank],
            send_sem=square_send,
            recv_sem=square_recv,
            device_id={"tp": peer},
            device_id_type=MESH,
        ).start()
        return carry

    lax.fori_loop(1, ranks, tell, 0)
    for h in range(heads):
        span = slice(h * HEAD_DIM, (h + 1) * HEAD_DIM)
        new_state_ref[span] = (
            final[h : h + 1, :] * state[span].astype(jnp.float32) + fresh[span]
        ).astype(jnp.bfloat16)

    stores[2].start()
    part = square_in.at[pl.ds(0, ranks - 1)]
    pltpu.make_async_copy(part, part, square_recv).wait()
    mean = jnp.sum(square_in[...], axis=0) / (x_ref.shape[1] * ranks)
    scale = lax.rsqrt(mean + EPSILON)
    scale = jnp.transpose(jnp.broadcast_to(scale[:1], (tokens, tokens)))
    live = row_id < length
    scale = jnp.where(live, scale, 0.0)
    for pair in range(tiles):
        span = slice(pair * LANES, (pair + 1) * LANES)
        mixer_ref[:, span] = (raw[:, span] * scale * gain_ref[:, span]).astype(jnp.bfloat16)

    stores[0].start()

    cached = cached_len_ref[source_ref[me]]
    keys_new = new_ref[:, :LANES]
    values_new = new_ref[:, LANES:]
    arrived(kv_in, 3)
    keys = []
    values = []
    for page in range(instances // 2):
        keys.append(kv_in[2 * page])
        values.append(kv_in[2 * page + 1])
    keys = jnp.concatenate(keys, axis=0)
    values = jnp.concatenate(values, axis=0)
    cache_rows = keys.shape[0]
    key_id = lax.broadcasted_iota(jnp.int32, (tokens, cache_rows), 1)
    seen = key_id < cached
    for head in range(tiles):
        span = slice(head * LANES, (head + 1) * LANES)
        query = q_ref[:, span]
        old = lax.dot_general(
            query, keys, (((1,), (1,)), ((), ())), preferred_element_type=jnp.float32
        )
        new = lax.dot_general(
            query, keys_new, (((1,), (1,)), ((), ())), preferred_element_type=jnp.float32
        )
        old = jnp.where(seen, old, FAR_BELOW)
        new = jnp.where(lower, new, FAR_BELOW)
        top = jnp.maximum(
            jnp.max(old, axis=1, keepdims=True), jnp.max(new, axis=1, keepdims=True)
        )
        old = jnp.exp((old - top) * SCORE_SCALE)
        new = jnp.exp((new - top) * SCORE_SCALE)
        weight = jnp.sum(old, axis=1, keepdims=True) + jnp.sum(new, axis=1, keepdims=True)
        out = jnp.dot(
            old.astype(jnp.bfloat16), values, preferred_element_type=jnp.float32
        ) + jnp.dot(new.astype(jnp.bfloat16), values_new, preferred_element_type=jnp.float32)
        attn_ref[:, span] = jnp.where(live, out / weight, 0.0).astype(jnp.bfloat16)

    stores[1].start()
    sent(state_out, 0)
    sent(kv_out, 1)
    sent(state_fwd, 2)
    sent(kv_fwd, 3)
    part = square_in.at[pl.ds(0, ranks - 1)]
    pltpu.make_async_copy(part, part, square_send).wait()
    for store in stores:
        store.wait()


def on_device(
    instances,
    ranks,
    cached_state,
    kv_pool,
    page_table,
    cached_len,
    source_session,
    turn_len,
    x_inner,
    gate_z,
    b_proj,
    c_proj,
    step_size,
    decay_rate,
    skip_gain,
    norm_gain,
    queries,
    new_kv,
):
    stores, rows, width = cached_state.shape
    piece = (instances, PAGE, LANES)
    tokens, inner = x_inner.shape
    hbm = pl.BlockSpec(memory_space=pltpu.HBM)
    operands = (
        (source_session, pltpu.SMEM),
        (page_table, pltpu.SMEM),
        (cached_state.reshape(stores, instances, PAGE, width), pltpu.VMEM),
        (kv_pool, pltpu.VMEM),
        (turn_len, pltpu.SMEM),
        (decay_rate, pltpu.SMEM),
        (skip_gain, pltpu.SMEM),
        (x_inner, pltpu.VMEM),
        (b_proj, pltpu.VMEM),
        (c_proj, pltpu.VMEM),
        (step_size, pltpu.VMEM),
        (gate_z, pltpu.VMEM),
        (norm_gain.reshape(1, inner), pltpu.VMEM),
        (cached_len, pltpu.SMEM),
        (queries, pltpu.VMEM),
        (new_kv, pltpu.VMEM),
    )
    results = (
        jax.ShapeDtypeStruct((tokens, inner), jnp.bfloat16),
        jax.ShapeDtypeStruct((tokens, inner), jnp.bfloat16),
        jax.ShapeDtypeStruct((rows, width), jnp.bfloat16),
    )
    mixer_out, attn_out, new_state = pl.pallas_call(
        functools.partial(serve_kernel, instances, ranks),
        out_shape=results,
        in_specs=[hbm] * N_OPERANDS,
        out_specs=(pl.BlockSpec(memory_space=pl.ANY),) * N_OUTPUTS,
        scratch_shapes=[space(array.shape, array.dtype) for array, space in operands]
        + [pltpu.VMEM(result.shape, result.dtype) for result in results]
        + [pltpu.VMEM(piece, jnp.bfloat16)] * 8
        + [
            pltpu.VMEM((8, LANES), jnp.float32),
            pltpu.VMEM((ranks, 8, LANES), jnp.float32),
            pltpu.VMEM((tokens, inner), jnp.float32),
            pltpu.VMEM((tokens, inner), jnp.float32),
            pltpu.VMEM((tokens, inner), jnp.float32),
            pltpu.VMEM((rows, width), jnp.float32),
            pltpu.SemaphoreType.DMA((4,)),
            pltpu.SemaphoreType.DMA((4,)),
            pltpu.SemaphoreType.DMA,
            pltpu.SemaphoreType.DMA,
            pltpu.SemaphoreType.DMA((N_OPERANDS,)),
            pltpu.SemaphoreType.DMA((N_OUTPUTS,)),
        ],
        compiler_params=pltpu.CompilerParams(
            collective_id=0, has_side_effects=True, vmem_limit_bytes=48 * 1024 * 1024
        ),
    )(*((array if array.size == 1 else pltpu.with_memory_space_constraint(array, pltpu.HBM)) for array, _ in operands))
    return (mixer_out, attn_out, new_state.reshape(1, rows, width))


def solution(mesh):
    in_specs = (
        P("inst", "tp", None),
        P("inst", None, "tp"),
        P("inst", None),
        P(),
        P(),
        P("inst"),
        P("inst", "tp"),
        P("inst", "tp"),
        P("inst", "tp"),
        P("inst", "tp"),
        P("tp", "inst"),
        P("tp"),
        P("tp"),
        P("tp"),
        P("inst", "tp"),
        P("inst", "tp"),
    )
    out_specs = (P("inst", "tp"), P("inst", "tp"), P("inst", "tp", None))
    body = functools.partial(on_device, mesh.shape["inst"], mesh.shape["tp"])
    return jax.shard_map(
        body, mesh=mesh, in_specs=in_specs, out_specs=out_specs, check_vma=False
    )
```

```python
import functools

import jax
import jax.numpy as jnp
from jax import lax
from jax.experimental import pallas as pl
from jax.experimental.pallas import tpu as pltpu
from jax.sharding import PartitionSpec as P

MESH = pl.DeviceIdType.MESH
HEAD_DIM = 64
LANES = 128
PAGE = 16
EPSILON = 1e-05
SCORE_SCALE = 128 ** (-0.5)
FAR_BELOW = -1e30
N_OPERANDS = 16
N_OUTPUTS = 2
ROW = 4


def serve_kernel(
    instances,
    ranks,
    *refs,
):
    operands, refs = refs[:N_OPERANDS], refs[N_OPERANDS:]
    outputs, refs = refs[:N_OUTPUTS], refs[N_OUTPUTS:]
    held, refs = refs[:N_OPERANDS], refs[N_OPERANDS:]
    (
        source_ref,
        page_ref,
        state_ref,
        kv_ref,
        turn_len_ref,
        rate_ref,
        skip_ref,
        x_ref,
        b_ref,
        c_ref,
        dt_ref,
        z_ref,
        gain_ref,
        cached_len_ref,
        q_ref,
        new_ref,
    ) = held
    rows_ref, new_state_ref = outputs
    mixer_ref, attn_ref = rows_ref.at[0], rows_ref.at[1]
    (
    state_out,
    state_mid,
    state_fwd,
    state_in,
    kv_out,
    kv_mid,
    kv_fwd,
    kv_in,
    square_out,
    square_in,
    raw,
    reach,
    silu,
    fresh,
    send_sem,
    recv_sem,
    square_send,
    square_recv,
    fetch_sem,
    best,
    total_weight,
    partial_out,
    ) = refs
    me = lax.axis_index("inst")
    rank = lax.axis_index("tp")
    others = instances - 1
    barrier = pltpu.get_barrier_semaphore()
    fetches = [
        pltpu.make_async_copy(operands[i], held[i], fetch_sem.at[i])
        for i in range(N_OPERANDS)
    ]
    for fetch in fetches[:4]:
        fetch.start()

    half = instances // 2
    side = me // half
    lane = me % ROW

    def around(k):
        return lax.rem(me + instances + (k + 2) // 2 * (1 - 2 * (k % 2)), instances)

    def hail(peer):
        pl.semaphore_signal(barrier, inc=1, device_id=peer, device_id_type=MESH)

    def greet(k, carry):
        hail({"inst": around(k)})
        return carry

    lax.fori_loop(0, others, greet, 0, unroll=7)

    def greet_rank(k, carry):
        hail({"tp": lax.rem(rank + k, ranks)})
        return carry

    lax.fori_loop(1, ranks, greet_rank, 0, unroll=7)

    for fetch in fetches[4:]:
        fetch.start()
    fetches[0].wait()

    def find(d, found):
        g = source_ref[d]
        return found + jnp.where(lax.shift_right_logical(g, 1) == me, g & 1, 0)

    slot = lax.fori_loop(0, instances, find, jnp.int32(0), unroll=8)
    fetches[1].wait()
    fetches[2].wait()
    state_out[...] = state_ref[slot]
    fetches[3].wait()
    for page in range(instances // 2):
        rows = kv_ref[page_ref[slot, page]]
        kv_out[2 * page] = rows[:, :LANES]
        kv_out[2 * page + 1] = rows[:, LANES:]

    def spread(out, mid, phase):
        def send(k, carry):
            peer = around(k)
            pltpu.make_async_remote_copy(
                src_ref=out.at[peer],
                dst_ref=mid.at[me],
                send_sem=send_sem.at[phase],
                recv_sem=recv_sem.at[phase],
                device_id={"inst": peer},
                device_id_type=MESH,
            ).start()
            return carry

        lax.fori_loop(0, others, send, 0, unroll=7)

    def in_turn(k):
        return k // ROW * ROW + (lane + k) % ROW

    def collect(mid, fwd, arrive, phase, recv, target):
        def send(k, carry):
            peer = target(k)

            @pl.when(peer != me)
            def _():
                holder = lax.shift_right_logical(source_ref[peer], 1)
                fwd[peer] = mid[holder]
                pltpu.make_async_remote_copy(
                    src_ref=fwd.at[peer],
                    dst_ref=arrive.at[me],
                    send_sem=send_sem.at[phase],
                    recv_sem=recv_sem.at[recv],
                    device_id={"inst": peer},
                    device_id_type=MESH,
                ).start()

            return carry

        lax.fori_loop(0, instances, send, 0)
        arrive[me] = mid[lax.shift_right_logical(source_ref[me], 1)]

    def arrived(buffer, recv, count):
        part = buffer.at[pl.ds(0, count)]
        pltpu.make_async_copy(part, part, recv_sem.at[recv]).wait()

    def sent(buffer, phase):
        part = buffer.at[pl.ds(0, others)]
        pltpu.make_async_copy(part, part, send_sem.at[phase]).wait()

    pl.semaphore_wait(barrier, others + ranks - 1)
    spread(state_out, state_mid, 0)
    spread(kv_out, kv_mid, 1)
    state_mid[me] = state_out[me]
    kv_mid[me] = kv_out[me]

    for fetch in fetches[4:]:
        fetch.wait()
    length = turn_len_ref[0]
    tokens = x_ref.shape[0]
    heads = dt_ref.shape[0]
    tiles = x_ref.shape[1] // LANES
    row_id = lax.broadcasted_iota(jnp.int32, (tokens, tokens), 0)
    col_id = lax.broadcasted_iota(jnp.int32, (tokens, tokens), 1)
    lower = row_id >= col_id
    first_head = col_id < HEAD_DIM
    head_id = lax.broadcasted_iota(jnp.int32, (heads, tokens), 0)
    token_id = lax.broadcasted_iota(jnp.int32, (heads, tokens), 1)
    rate = jnp.zeros((heads, tokens), jnp.float32)
    for h in range(heads):
        rate = jnp.where(head_id == h, rate_ref[h], rate)
    dt = jnp.where(token_id < length, dt_ref[...], 0.0)
    log_decay = -dt * rate
    cumulative = lax.dot_general(
        log_decay,
        lower.astype(jnp.float32),
        (((1,), (1,)), ((), ())),
        precision=lax.Precision.HIGHEST,
        preferred_element_type=jnp.float32,
    )
    last = jnp.broadcast_to(cumulative[:, tokens - 1 : tokens], (heads, tokens))
    tail = jnp.exp(last - cumulative) * dt
    final = jnp.exp(last)
    stacked = jnp.concatenate(
        [
            cumulative,
            jnp.exp(cumulative),
            tail,
            jnp.zeros((tokens - 3 * heads, tokens), jnp.float32),
        ],
        axis=0,
    )
    columns = jnp.transpose(stacked)

    def column(index):
        return jnp.broadcast_to(columns[:, index : index + 1], (tokens, tokens))

    b = b_ref[...]
    c = c_ref[...]
    b_wide = b.astype(jnp.float32)
    products = lax.dot_general(
        c, b, (((1,), (1,)), ((), ())), preferred_element_type=jnp.float32
    )
    for pair in range(tiles):
        span = slice(pair * LANES, (pair + 1) * LANES)
        x = x_ref[:, span]
        parts = []
        mixed = []
        for h in (2 * pair, 2 * pair + 1):
            differ = column(h) - cumulative[h : h + 1, :]
            decay = jnp.exp(jnp.where(lower, differ, FAR_BELOW))
            weights = (products * decay * dt[h : h + 1, :]).astype(jnp.bfloat16)
            parts.append(jnp.dot(weights, x, preferred_element_type=jnp.float32))
            mixed.append((column(2 * heads + h) * b_wide).astype(jnp.bfloat16))
        gain = jnp.where(first_head, skip_ref[2 * pair], skip_ref[2 * pair + 1])
        raw[:, span] = jnp.where(first_head, parts[0], parts[1]) + gain * x.astype(
            jnp.float32
        )
        reach[:, span] = jnp.where(
            first_head, column(heads + 2 * pair), column(heads + 2 * pair + 1)
        )
        z = z_ref[:, span].astype(jnp.float32)
        silu[:, span] = z / (1.0 + jnp.exp(-z))
        both = lax.dot_general(
            x,
            jnp.concatenate(mixed, axis=1),
            (((0,), (0,)), ((), ())),
            preferred_element_type=jnp.float32,
        )
        top = pair * LANES
        fresh[top : top + HEAD_DIM] = both[:HEAD_DIM, :LANES]
        fresh[top + HEAD_DIM : top + LANES] = both[HEAD_DIM:, LANES:]

    live = row_id < length
    scores = functools.partial(
        lax.dot_general,
        dimension_numbers=(((1,), (1,)), ((), ())),
        preferred_element_type=jnp.float32,
    )

    def attend(head, keys, values, seen):
        old = jnp.where(seen, scores(q_ref[:, head * LANES : (head + 1) * LANES], keys), FAR_BELOW)
        top = jnp.max(old, axis=1, keepdims=True)
        old = jnp.exp((old - top) * SCORE_SCALE)
        weight = jnp.sum(old, axis=1, keepdims=True)
        out = jnp.dot(old.astype(jnp.bfloat16), values, preferred_element_type=jnp.float32)
        wide = (tokens, LANES)
        return jnp.broadcast_to(top, wide), jnp.broadcast_to(weight, wide), out

    def merge(one, two):
        top = jnp.maximum(one[0], two[0])
        left = jnp.exp((one[0] - top) * SCORE_SCALE)
        right = jnp.exp((two[0] - top) * SCORE_SCALE)
        return top, one[1] * left + two[1] * right, one[2] * left + two[2] * right

    keys_new = new_ref[:, :LANES]
    values_new = new_ref[:, LANES:]
    for head in range(tiles):
        span = slice(head * LANES, (head + 1) * LANES)
        best[:, span], total_weight[:, span], partial_out[:, span] = attend(
            head, keys_new, values_new, lower
        )

    arrived(state_mid, 0, others)
    collect(state_mid, state_fwd, state_in, 2, 2, in_turn)
    arrived(kv_mid, 1, others)

    @pl.when(side == 0)
    def _():
        collect(kv_mid, kv_fwd, kv_in, 3, 3, in_turn)

    @pl.when(side == 1)
    def _():
        collect(kv_mid, kv_fwd, kv_in, 3, 4, in_turn)

    arrived(state_in, 2, others)
    state = state_in[...].reshape(x_ref.shape[1], LANES)
    total = jnp.zeros((tokens, LANES), jnp.float32)
    for pair in range(tiles):
        span = slice(pair * LANES, (pair + 1) * LANES)
        carried = lax.dot_general(
            c, state[span], (((1,), (1,)), ((), ())), preferred_element_type=jnp.float32
        )
        gated = (raw[:, span] + reach[:, span] * carried) * silu[:, span]
        raw[:, span] = gated
        total = total + gated * gated
    squares = jnp.sum(jnp.transpose(total), axis=0, keepdims=True)
    square_out[...] = jnp.broadcast_to(squares, square_out.shape)
    square_in[rank] = jnp.broadcast_to(squares, square_out.shape)

    def tell(k, carry):
        peer = lax.rem(rank + k, ranks)
        pltpu.make_async_remote_copy(
            src_ref=square_out,
            dst_ref=square_in.at[rank],
            send_sem=square_send,
            recv_sem=square_recv,
            device_id={"tp": peer},
            device_id_type=MESH,
        ).start()
        return carry

    lax.fori_loop(1, ranks, tell, 0)
    for h in range(heads):
        span = slice(h * HEAD_DIM, (h + 1) * HEAD_DIM)
        new_state_ref[span] = (
            final[h : h + 1, :] * state[span].astype(jnp.float32) + fresh[span]
        ).astype(jnp.bfloat16)

    part = square_in.at[pl.ds(0, ranks - 1)]
    pltpu.make_async_copy(part, part, square_recv).wait()
    mean = jnp.sum(square_in[...], axis=0) / (x_ref.shape[1] * ranks)
    scale = lax.rsqrt(mean + EPSILON)
    scale = jnp.transpose(jnp.broadcast_to(scale[:1], (tokens, tokens)))
    scale = jnp.where(live, scale, 0.0)
    for pair in range(tiles):
        span = slice(pair * LANES, (pair + 1) * LANES)
        mixer_ref[:, span] = (raw[:, span] * scale * gain_ref[:, span]).astype(jnp.bfloat16)


    cached = cached_len_ref[source_ref[me]]
    key_id = lax.broadcasted_iota(jnp.int32, (tokens, half // 2 * PAGE), 1)
    for origin in range(2):

        @pl.when(side == origin)
        def _():
            arrived(kv_in, 3 + origin, half - 1)

        @pl.when(side != origin)
        def _():
            arrived(kv_in, 3 + origin, half)

        first = origin * half
        keys = jnp.concatenate([kv_in[first + 2 * p] for p in range(half // 2)], axis=0)
        values = jnp.concatenate(
            [kv_in[first + 2 * p + 1] for p in range(half // 2)], axis=0
        )
        seen = key_id + first // 2 * PAGE < cached
        for head in range(tiles):
            span = slice(head * LANES, (head + 1) * LANES)
            top, weight, out = merge(
                (best[:, span], total_weight[:, span], partial_out[:, span]),
                attend(head, keys, values, seen),
            )
            if origin == 0:
                best[:, span], total_weight[:, span], partial_out[:, span] = top, weight, out
            else:
                attn_ref[:, span] = jnp.where(live, out / weight, 0.0).astype(jnp.bfloat16)

    sent(state_out, 0)
    sent(kv_out, 1)
    sent(state_fwd, 2)
    sent(kv_fwd, 3)
    part = square_in.at[pl.ds(0, ranks - 1)]
    pltpu.make_async_copy(part, part, square_send).wait()


def on_device(
    instances,
    ranks,
    cached_state,
    kv_pool,
    page_table,
    cached_len,
    source_session,
    turn_len,
    x_inner,
    gate_z,
    b_proj,
    c_proj,
    step_size,
    decay_rate,
    skip_gain,
    norm_gain,
    queries,
    new_kv,
):
    stores, rows, width = cached_state.shape
    piece = (instances, PAGE, LANES)
    tokens, inner = x_inner.shape
    hbm = pl.BlockSpec(memory_space=pltpu.HBM)
    operands = (
        (source_session, pltpu.SMEM),
        (page_table, pltpu.SMEM),
        (cached_state.reshape(stores, instances, PAGE, width), pltpu.VMEM),
        (kv_pool, pltpu.VMEM),
        (turn_len, pltpu.SMEM),
        (decay_rate, pltpu.SMEM),
        (skip_gain, pltpu.SMEM),
        (x_inner, pltpu.VMEM),
        (b_proj, pltpu.VMEM),
        (c_proj, pltpu.VMEM),
        (step_size, pltpu.VMEM),
        (gate_z, pltpu.VMEM),
        (norm_gain.reshape(1, inner), pltpu.VMEM),
        (cached_len, pltpu.SMEM),
        (queries, pltpu.VMEM),
        (new_kv, pltpu.VMEM),
    )
    results = (
        jax.ShapeDtypeStruct((2, tokens, inner), jnp.bfloat16),
        jax.ShapeDtypeStruct((rows, width), jnp.bfloat16),
    )
    token_rows, new_state = pl.pallas_call(
        functools.partial(serve_kernel, instances, ranks),
        out_shape=results,
        in_specs=[hbm] * N_OPERANDS,
        out_specs=(pl.BlockSpec(memory_space=pltpu.VMEM),) * N_OUTPUTS,
        scratch_shapes=[space(array.shape, array.dtype) for array, space in operands]
        + [pltpu.VMEM(piece, jnp.bfloat16)] * 8
        + [
            pltpu.VMEM((8, LANES), jnp.float32),
            pltpu.VMEM((ranks, 8, LANES), jnp.float32),
            pltpu.VMEM((tokens, inner), jnp.float32),
            pltpu.VMEM((tokens, inner), jnp.float32),
            pltpu.VMEM((tokens, inner), jnp.float32),
            pltpu.VMEM((rows, width), jnp.float32),
            pltpu.SemaphoreType.DMA((4,)),
            pltpu.SemaphoreType.DMA((5,)),
            pltpu.SemaphoreType.DMA,
            pltpu.SemaphoreType.DMA,
            pltpu.SemaphoreType.DMA((N_OPERANDS,)),
            pltpu.VMEM((tokens, inner), jnp.float32),
            pltpu.VMEM((tokens, inner), jnp.float32),
            pltpu.VMEM((tokens, inner), jnp.float32),
        ],
        compiler_params=pltpu.CompilerParams(
            collective_id=0, has_side_effects=True, vmem_limit_bytes=48 * 1024 * 1024
        ),
    )(*((array if array.size == 1 else pltpu.with_memory_space_constraint(array, pltpu.HBM)) for array, _ in operands))
    mixer_out, attn_out = token_rows[0], token_rows[1]
    return (mixer_out, attn_out, new_state.reshape(1, rows, width))


def solution(mesh):
    in_specs = (
        P("inst", "tp", None),
        P("inst", None, "tp"),
        P("inst", None),
        P(),
        P(),
        P("inst"),
        P("inst", "tp"),
        P("inst", "tp"),
        P("inst", "tp"),
        P("inst", "tp"),
        P("tp", "inst"),
        P("tp"),
        P("tp"),
        P("tp"),
        P("inst", "tp"),
        P("inst", "tp"),
    )
    out_specs = (P("inst", "tp"), P("inst", "tp"), P("inst", "tp", None))
    body = functools.partial(on_device, mesh.shape["inst"], mesh.shape["tp"])
    return jax.shard_map(
        body, mesh=mesh, in_specs=in_specs, out_specs=out_specs, check_vma=False
    )
```

```python
import functools

import jax
import jax.numpy as jnp
from jax import lax
from jax.experimental import pallas as pl
from jax.experimental.pallas import tpu as pltpu
from jax.sharding import PartitionSpec as P

MESH = pl.DeviceIdType.MESH
HEAD_DIM = 64
LANES = 128
PAGE = 16
EPSILON = 1e-05
SCORE_SCALE = 128 ** (-0.5)
FAR_BELOW = -1e30
N_OPERANDS = 16
N_OUTPUTS = 2
ROW = 4


def serve_kernel(
    instances,
    ranks,
    *refs,
):
    operands, refs = refs[:N_OPERANDS], refs[N_OPERANDS:]
    outputs, refs = refs[:N_OUTPUTS], refs[N_OUTPUTS:]
    held, refs = refs[:N_OPERANDS], refs[N_OPERANDS:]
    (
        source_ref,
        page_ref,
        state_ref,
        kv_ref,
        turn_len_ref,
        rate_ref,
        skip_ref,
        x_ref,
        b_ref,
        c_ref,
        dt_ref,
        z_ref,
        gain_ref,
        cached_len_ref,
        q_ref,
        new_ref,
    ) = held
    rows_ref, new_state_ref = outputs
    mixer_ref, attn_ref = rows_ref.at[0], rows_ref.at[1]
    (
    state_out,
    state_mid,
    state_fwd,
    state_in,
    kv_out,
    kv_mid,
    kv_fwd,
    kv_in,
    square_out,
    square_in,
    raw,
    reach,
    silu,
    fresh,
    send_sem,
    recv_sem,
    square_send,
    square_recv,
    fetch_sem,
    best,
    total_weight,
    partial_out,
    ) = refs
    me = lax.axis_index("inst")
    rank = lax.axis_index("tp")
    others = instances - 1
    barrier = pltpu.get_barrier_semaphore()
    fetches = [
        pltpu.make_async_copy(operands[i], held[i], fetch_sem.at[i])
        for i in range(N_OPERANDS)
    ]
    for fetch in fetches[:4]:
        fetch.start()

    half = instances // 2
    side = me // half
    lane = me % ROW

    def around(k):
        return lax.rem(me + instances + (k + 2) // 2 * (1 - 2 * (k % 2)), instances)

    def hail(peer):
        pl.semaphore_signal(barrier, inc=1, device_id=peer, device_id_type=MESH)

    def greet(k, carry):
        hail({"inst": around(others - 1 - k)})
        return carry

    lax.fori_loop(0, others, greet, 0, unroll=7)

    def greet_rank(k, carry):
        hail({"tp": lax.rem(rank + k, ranks)})
        return carry

    lax.fori_loop(1, ranks, greet_rank, 0, unroll=7)

    for fetch in fetches[4:]:
        fetch.start()
    fetches[0].wait()

    def find(d, found):
        g = source_ref[d]
        return found + jnp.where(lax.shift_right_logical(g, 1) == me, g & 1, 0)

    slot = lax.fori_loop(0, instances, find, jnp.int32(0), unroll=8)
    fetches[1].wait()
    fetches[2].wait()
    state_out[...] = state_ref[slot]
    fetches[3].wait()
    for page in range(instances // 2):
        rows = kv_ref[page_ref[slot, page]]
        kv_out[2 * page] = rows[:, :LANES]
        kv_out[2 * page + 1] = rows[:, LANES:]

    def outward(k):
        return around(others - 1 - k)

    def spread(out, mid, phase):
        def send(k, carry):
            peer = outward(k)
            pltpu.make_async_remote_copy(
                src_ref=out.at[peer],
                dst_ref=mid.at[me],
                send_sem=send_sem.at[phase],
                recv_sem=recv_sem.at[phase],
                device_id={"inst": peer},
                device_id_type=MESH,
            ).start()
            return carry

        lax.fori_loop(0, others, send, 0, unroll=7)

    def in_turn(k):
        return k // ROW * ROW + (lane + k) % ROW

    def collect(mid, fwd, arrive, phase, recv, target):
        def send(k, carry):
            peer = target(k)

            @pl.when(peer != me)
            def _():
                holder = lax.shift_right_logical(source_ref[peer], 1)
                fwd[peer] = mid[holder]
                pltpu.make_async_remote_copy(
                    src_ref=fwd.at[peer],
                    dst_ref=arrive.at[me],
                    send_sem=send_sem.at[phase],
                    recv_sem=recv_sem.at[recv],
                    device_id={"inst": peer},
                    device_id_type=MESH,
                ).start()

            return carry

        lax.fori_loop(0, instances, send, 0)
        arrive[me] = mid[lax.shift_right_logical(source_ref[me], 1)]

    def arrived(buffer, recv, count):
        part = buffer.at[pl.ds(0, count)]
        pltpu.make_async_copy(part, part, recv_sem.at[recv]).wait()

    def sent(buffer, phase):
        part = buffer.at[pl.ds(0, others)]
        pltpu.make_async_copy(part, part, send_sem.at[phase]).wait()

    pl.semaphore_wait(barrier, others + ranks - 1)
    spread(state_out, state_mid, 0)
    spread(kv_out, kv_mid, 1)
    state_mid[me] = state_out[me]
    kv_mid[me] = kv_out[me]

    for fetch in fetches[4:]:
        fetch.wait()
    length = turn_len_ref[0]
    tokens = x_ref.shape[0]
    heads = dt_ref.shape[0]
    tiles = x_ref.shape[1] // LANES
    row_id = lax.broadcasted_iota(jnp.int32, (tokens, tokens), 0)
    col_id = lax.broadcasted_iota(jnp.int32, (tokens, tokens), 1)
    lower = row_id >= col_id
    first_head = col_id < HEAD_DIM
    head_id = lax.broadcasted_iota(jnp.int32, (heads, tokens), 0)
    token_id = lax.broadcasted_iota(jnp.int32, (heads, tokens), 1)
    rate = jnp.zeros((heads, tokens), jnp.float32)
    for h in range(heads):
        rate = jnp.where(head_id == h, rate_ref[h], rate)
    dt = jnp.where(token_id < length, dt_ref[...], 0.0)
    log_decay = -dt * rate
    cumulative = lax.dot_general(
        log_decay,
        lower.astype(jnp.float32),
        (((1,), (1,)), ((), ())),
        precision=lax.Precision.HIGHEST,
        preferred_element_type=jnp.float32,
    )
    last = jnp.broadcast_to(cumulative[:, tokens - 1 : tokens], (heads, tokens))
    tail = jnp.exp(last - cumulative) * dt
    final = jnp.exp(last)
    stacked = jnp.concatenate(
        [
            cumulative,
            jnp.exp(cumulative),
            tail,
            jnp.zeros((tokens - 3 * heads, tokens), jnp.float32),
        ],
        axis=0,
    )
    columns = jnp.transpose(stacked)

    def column(index):
        return jnp.broadcast_to(columns[:, index : index + 1], (tokens, tokens))

    b = b_ref[...]
    c = c_ref[...]
    b_wide = b.astype(jnp.float32)
    products = lax.dot_general(
        c, b, (((1,), (1,)), ((), ())), preferred_element_type=jnp.float32
    )
    for pair in range(tiles):
        span = slice(pair * LANES, (pair + 1) * LANES)
        x = x_ref[:, span]
        parts = []
        mixed = []
        for h in (2 * pair, 2 * pair + 1):
            differ = column(h) - cumulative[h : h + 1, :]
            decay = jnp.exp(jnp.where(lower, differ, FAR_BELOW))
            weights = (products * decay * dt[h : h + 1, :]).astype(jnp.bfloat16)
            parts.append(jnp.dot(weights, x, preferred_element_type=jnp.float32))
            mixed.append((column(2 * heads + h) * b_wide).astype(jnp.bfloat16))
        gain = jnp.where(first_head, skip_ref[2 * pair], skip_ref[2 * pair + 1])
        raw[:, span] = jnp.where(first_head, parts[0], parts[1]) + gain * x.astype(
            jnp.float32
        )
        reach[:, span] = jnp.where(
            first_head, column(heads + 2 * pair), column(heads + 2 * pair + 1)
        )
        z = z_ref[:, span].astype(jnp.float32)
        silu[:, span] = z / (1.0 + jnp.exp(-z))
        both = lax.dot_general(
            x,
            jnp.concatenate(mixed, axis=1),
            (((0,), (0,)), ((), ())),
            preferred_element_type=jnp.float32,
        )
        top = pair * LANES
        fresh[top : top + HEAD_DIM] = both[:HEAD_DIM, :LANES]
        fresh[top + HEAD_DIM : top + LANES] = both[HEAD_DIM:, LANES:]

    live = row_id < length
    scores = functools.partial(
        lax.dot_general,
        dimension_numbers=(((1,), (1,)), ((), ())),
        preferred_element_type=jnp.float32,
    )

    def attend(head, keys, values, seen):
        old = jnp.where(seen, scores(q_ref[:, head * LANES : (head + 1) * LANES], keys), FAR_BELOW)
        top = jnp.max(old, axis=1, keepdims=True)
        old = jnp.exp((old - top) * SCORE_SCALE)
        weight = jnp.sum(old, axis=1, keepdims=True)
        out = jnp.dot(old.astype(jnp.bfloat16), values, preferred_element_type=jnp.float32)
        wide = (tokens, LANES)
        return jnp.broadcast_to(top, wide), jnp.broadcast_to(weight, wide), out

    def merge(one, two):
        top = jnp.maximum(one[0], two[0])
        left = jnp.exp((one[0] - top) * SCORE_SCALE)
        right = jnp.exp((two[0] - top) * SCORE_SCALE)
        return top, one[1] * left + two[1] * right, one[2] * left + two[2] * right

    keys_new = new_ref[:, :LANES]
    values_new = new_ref[:, LANES:]
    for head in range(tiles):
        span = slice(head * LANES, (head + 1) * LANES)
        best[:, span], total_weight[:, span], partial_out[:, span] = attend(
            head, keys_new, values_new, lower
        )

    arrived(state_mid, 0, others)
    collect(state_mid, state_fwd, state_in, 2, 2, in_turn)
    arrived(kv_mid, 1, others)

    @pl.when(side == 0)
    def _():
        collect(kv_mid, kv_fwd, kv_in, 3, 3, in_turn)

    @pl.when(side == 1)
    def _():
        collect(kv_mid, kv_fwd, kv_in, 3, 4, in_turn)

    arrived(state_in, 2, others)
    state = state_in[...].reshape(x_ref.shape[1], LANES)
    total = jnp.zeros((tokens, LANES), jnp.float32)
    for pair in range(tiles):
        span = slice(pair * LANES, (pair + 1) * LANES)
        carried = lax.dot_general(
            c, state[span], (((1,), (1,)), ((), ())), preferred_element_type=jnp.float32
        )
        gated = (raw[:, span] + reach[:, span] * carried) * silu[:, span]
        raw[:, span] = gated
        total = total + gated * gated
    squares = jnp.sum(jnp.transpose(total), axis=0, keepdims=True)
    square_out[...] = jnp.broadcast_to(squares, square_out.shape)
    square_in[rank] = jnp.broadcast_to(squares, square_out.shape)

    def tell(k, carry):
        peer = lax.rem(rank + k, ranks)
        pltpu.make_async_remote_copy(
            src_ref=square_out,
            dst_ref=square_in.at[rank],
            send_sem=square_send,
            recv_sem=square_recv,
            device_id={"tp": peer},
            device_id_type=MESH,
        ).start()
        return carry

    lax.fori_loop(1, ranks, tell, 0)
    for h in range(heads):
        span = slice(h * HEAD_DIM, (h + 1) * HEAD_DIM)
        new_state_ref[span] = (
            final[h : h + 1, :] * state[span].astype(jnp.float32) + fresh[span]
        ).astype(jnp.bfloat16)

    part = square_in.at[pl.ds(0, ranks - 1)]
    pltpu.make_async_copy(part, part, square_recv).wait()
    mean = jnp.sum(square_in[...], axis=0) / (x_ref.shape[1] * ranks)
    scale = lax.rsqrt(mean + EPSILON)
    scale = jnp.transpose(jnp.broadcast_to(scale[:1], (tokens, tokens)))
    scale = jnp.where(live, scale, 0.0)
    for pair in range(tiles):
        span = slice(pair * LANES, (pair + 1) * LANES)
        mixer_ref[:, span] = (raw[:, span] * scale * gain_ref[:, span]).astype(jnp.bfloat16)


    cached = cached_len_ref[source_ref[me]]
    key_id = lax.broadcasted_iota(jnp.int32, (tokens, half // 2 * PAGE), 1)
    for origin in range(2):

        @pl.when(side == origin)
        def _():
            arrived(kv_in, 3 + origin, half - 1)

        @pl.when(side != origin)
        def _():
            arrived(kv_in, 3 + origin, half)

        first = origin * half
        keys = jnp.concatenate([kv_in[first + 2 * p] for p in range(half // 2)], axis=0)
        values = jnp.concatenate(
            [kv_in[first + 2 * p + 1] for p in range(half // 2)], axis=0
        )
        seen = key_id + first // 2 * PAGE < cached
        for head in range(tiles):
            span = slice(head * LANES, (head + 1) * LANES)
            top, weight, out = merge(
                (best[:, span], total_weight[:, span], partial_out[:, span]),
                attend(head, keys, values, seen),
            )
            if origin == 0:
                best[:, span], total_weight[:, span], partial_out[:, span] = top, weight, out
            else:
                attn_ref[:, span] = jnp.where(live, out / weight, 0.0).astype(jnp.bfloat16)

    sent(state_out, 0)
    sent(kv_out, 1)
    sent(state_fwd, 2)
    sent(kv_fwd, 3)
    part = square_in.at[pl.ds(0, ranks - 1)]
    pltpu.make_async_copy(part, part, square_send).wait()


def on_device(
    instances,
    ranks,
    cached_state,
    kv_pool,
    page_table,
    cached_len,
    source_session,
    turn_len,
    x_inner,
    gate_z,
    b_proj,
    c_proj,
    step_size,
    decay_rate,
    skip_gain,
    norm_gain,
    queries,
    new_kv,
):
    stores, rows, width = cached_state.shape
    piece = (instances, PAGE, LANES)
    tokens, inner = x_inner.shape
    hbm = pl.BlockSpec(memory_space=pltpu.HBM)
    operands = (
        (source_session, pltpu.SMEM),
        (page_table, pltpu.SMEM),
        (cached_state.reshape(stores, instances, PAGE, width), pltpu.VMEM),
        (kv_pool, pltpu.VMEM),
        (turn_len, pltpu.SMEM),
        (decay_rate, pltpu.SMEM),
        (skip_gain, pltpu.SMEM),
        (x_inner, pltpu.VMEM),
        (b_proj, pltpu.VMEM),
        (c_proj, pltpu.VMEM),
        (step_size, pltpu.VMEM),
        (gate_z, pltpu.VMEM),
        (norm_gain.reshape(1, inner), pltpu.VMEM),
        (cached_len, pltpu.SMEM),
        (queries, pltpu.VMEM),
        (new_kv, pltpu.VMEM),
    )
    results = (
        jax.ShapeDtypeStruct((2, tokens, inner), jnp.bfloat16),
        jax.ShapeDtypeStruct((rows, width), jnp.bfloat16),
    )
    token_rows, new_state = pl.pallas_call(
        functools.partial(serve_kernel, instances, ranks),
        out_shape=results,
        in_specs=[hbm] * N_OPERANDS,
        out_specs=(pl.BlockSpec(memory_space=pltpu.VMEM),) * N_OUTPUTS,
        scratch_shapes=[space(array.shape, array.dtype) for array, space in operands]
        + [pltpu.VMEM(piece, jnp.bfloat16)] * 8
        + [
            pltpu.VMEM((8, LANES), jnp.float32),
            pltpu.VMEM((ranks, 8, LANES), jnp.float32),
            pltpu.VMEM((tokens, inner), jnp.float32),
            pltpu.VMEM((tokens, inner), jnp.float32),
            pltpu.VMEM((tokens, inner), jnp.float32),
            pltpu.VMEM((rows, width), jnp.float32),
            pltpu.SemaphoreType.DMA((4,)),
            pltpu.SemaphoreType.DMA((5,)),
            pltpu.SemaphoreType.DMA,
            pltpu.SemaphoreType.DMA,
            pltpu.SemaphoreType.DMA((N_OPERANDS,)),
            pltpu.VMEM((tokens, inner), jnp.float32),
            pltpu.VMEM((tokens, inner), jnp.float32),
            pltpu.VMEM((tokens, inner), jnp.float32),
        ],
        compiler_params=pltpu.CompilerParams(
            collective_id=0, has_side_effects=True, vmem_limit_bytes=48 * 1024 * 1024
        ),
    )(*((array if array.size == 1 else pltpu.with_memory_space_constraint(array, pltpu.HBM)) for array, _ in operands))
    mixer_out, attn_out = token_rows[0], token_rows[1]
    return (mixer_out, attn_out, new_state.reshape(1, rows, width))


def solution(mesh):
    in_specs = (
        P("inst", "tp", None),
        P("inst", None, "tp"),
        P("inst", None),
        P(),
        P(),
        P("inst"),
        P("inst", "tp"),
        P("inst", "tp"),
        P("inst", "tp"),
        P("inst", "tp"),
        P("tp", "inst"),
        P("tp"),
        P("tp"),
        P("tp"),
        P("inst", "tp"),
        P("inst", "tp"),
    )
    out_specs = (P("inst", "tp"), P("inst", "tp"), P("inst", "tp", None))
    body = functools.partial(on_device, mesh.shape["inst"], mesh.shape["tp"])
    return jax.shard_map(
        body, mesh=mesh, in_specs=in_specs, out_specs=out_specs, check_vma=False
    )
```

```python
import functools

import jax
import jax.numpy as jnp
from jax import lax
from jax.experimental import pallas as pl
from jax.experimental.pallas import tpu as pltpu
from jax.sharding import PartitionSpec as P

MESH = pl.DeviceIdType.MESH
HEAD_DIM = 64
LANES = 128
PAGE = 16
EPSILON = 1e-05
SCORE_SCALE = 128 ** (-0.5)
FAR_BELOW = -1e30
N_OPERANDS = 16
N_OUTPUTS = 2
ROW = 4


def serve_kernel(
    instances,
    ranks,
    *refs,
):
    operands, refs = refs[:N_OPERANDS], refs[N_OPERANDS:]
    outputs, refs = refs[:N_OUTPUTS], refs[N_OUTPUTS:]
    held, refs = refs[:N_OPERANDS], refs[N_OPERANDS:]
    (
        source_ref,
        page_ref,
        state_ref,
        kv_ref,
        turn_len_ref,
        rate_ref,
        skip_ref,
        x_ref,
        b_ref,
        c_ref,
        dt_ref,
        z_ref,
        gain_ref,
        cached_len_ref,
        q_ref,
        new_ref,
    ) = held
    rows_ref, new_state_ref = outputs
    mixer_ref, attn_ref = rows_ref.at[0], rows_ref.at[1]
    (
    state_out,
    state_mid,
    state_fwd,
    state_in,
    kv_out,
    kv_mid,
    kv_fwd,
    kv_in,
    square_out,
    square_in,
    raw,
    reach,
    silu,
    fresh,
    send_sem,
    recv_sem,
    square_send,
    square_recv,
    fetch_sem,
    best,
    total_weight,
    partial_out,
    ) = refs
    me = lax.axis_index("inst")
    rank = lax.axis_index("tp")
    others = instances - 1
    barrier = pltpu.get_barrier_semaphore()
    fetches = [
        pltpu.make_async_copy(operands[i], held[i], fetch_sem.at[i])
        for i in range(N_OPERANDS)
    ]
    for fetch in fetches[:4]:
        fetch.start()

    half = instances // 2
    side = me // half
    lane = me % ROW

    def around(k):
        return lax.rem(me + instances + (k + 2) // 2 * (1 - 2 * (k % 2)), instances)

    def hail(peer):
        pl.semaphore_signal(barrier, inc=1, device_id=peer, device_id_type=MESH)

    def greet(k, carry):
        hail({"inst": around(others - 1 - k)})
        return carry

    lax.fori_loop(0, others, greet, 0, unroll=21)

    def greet_rank(k, carry):
        hail({"tp": lax.rem(rank + k, ranks)})
        return carry

    lax.fori_loop(1, ranks, greet_rank, 0, unroll=21)

    fetches[0].wait()

    def find(d, found):
        g = source_ref[d]
        return found + jnp.where(lax.shift_right_logical(g, 1) == me, g & 1, 0)

    slot = lax.fori_loop(0, instances, find, jnp.int32(0), unroll=8)
    fetches[1].wait()
    fetches[2].wait()
    state_out[...] = state_ref[slot]
    fetches[3].wait()
    for page in range(instances // 2):
        rows = kv_ref[page_ref[slot, page]]
        kv_out[2 * page] = rows[:, :LANES]
        kv_out[2 * page + 1] = rows[:, LANES:]

    def outward(k):
        return around(others - 1 - k)

    def spread(out, mid, phase):
        def send(k, carry):
            peer = outward(k)
            pltpu.make_async_remote_copy(
                src_ref=out.at[peer],
                dst_ref=mid.at[me],
                send_sem=send_sem.at[phase],
                recv_sem=recv_sem.at[phase],
                device_id={"inst": peer},
                device_id_type=MESH,
            ).start()
            return carry

        lax.fori_loop(0, others, send, 0, unroll=21)

    def in_turn(k):
        return k // ROW * ROW + (lane + k) % ROW

    def collect(mid, fwd, arrive, phase, recv, target):
        def send(k, carry):
            peer = target(k)

            @pl.when(peer != me)
            def _():
                holder = lax.shift_right_logical(source_ref[peer], 1)
                fwd[peer] = mid[holder]
                pltpu.make_async_remote_copy(
                    src_ref=fwd.at[peer],
                    dst_ref=arrive.at[me],
                    send_sem=send_sem.at[phase],
                    recv_sem=recv_sem.at[recv],
                    device_id={"inst": peer},
                    device_id_type=MESH,
                ).start()

            return carry

        lax.fori_loop(0, instances, send, 0)
        arrive[me] = mid[lax.shift_right_logical(source_ref[me], 1)]

    def arrived(buffer, recv, count):
        part = buffer.at[pl.ds(0, count)]
        pltpu.make_async_copy(part, part, recv_sem.at[recv]).wait()

    def sent(buffer, phase):
        part = buffer.at[pl.ds(0, others)]
        pltpu.make_async_copy(part, part, send_sem.at[phase]).wait()

    pl.semaphore_wait(barrier, others + ranks - 1)
    spread(state_out, state_mid, 0)
    spread(kv_out, kv_mid, 1)
    for fetch in fetches[4:]:
        fetch.start()
    state_mid[me] = state_out[me]
    kv_mid[me] = kv_out[me]

    for fetch in fetches[4:]:
        fetch.wait()
    length = turn_len_ref[0]
    tokens = x_ref.shape[0]
    heads = dt_ref.shape[0]
    tiles = x_ref.shape[1] // LANES
    row_id = lax.broadcasted_iota(jnp.int32, (tokens, tokens), 0)
    col_id = lax.broadcasted_iota(jnp.int32, (tokens, tokens), 1)
    lower = row_id >= col_id
    first_head = col_id < HEAD_DIM
    head_id = lax.broadcasted_iota(jnp.int32, (heads, tokens), 0)
    token_id = lax.broadcasted_iota(jnp.int32, (heads, tokens), 1)
    rate = jnp.zeros((heads, tokens), jnp.float32)
    for h in range(heads):
        rate = jnp.where(head_id == h, rate_ref[h], rate)
    dt = jnp.where(token_id < length, dt_ref[...], 0.0)
    log_decay = -dt * rate
    cumulative = lax.dot_general(
        log_decay,
        lower.astype(jnp.float32),
        (((1,), (1,)), ((), ())),
        precision=lax.Precision.HIGHEST,
        preferred_element_type=jnp.float32,
    )
    last = jnp.broadcast_to(cumulative[:, tokens - 1 : tokens], (heads, tokens))
    tail = jnp.exp(last - cumulative) * dt
    final = jnp.exp(last)
    stacked = jnp.concatenate(
        [
            cumulative,
            jnp.exp(cumulative),
            tail,
            jnp.zeros((tokens - 3 * heads, tokens), jnp.float32),
        ],
        axis=0,
    )
    columns = jnp.transpose(stacked)

    def column(index):
        return jnp.broadcast_to(columns[:, index : index + 1], (tokens, tokens))

    b = b_ref[...]
    c = c_ref[...]
    b_wide = b.astype(jnp.float32)
    products = lax.dot_general(
        c, b, (((1,), (1,)), ((), ())), preferred_element_type=jnp.float32
    )
    for pair in range(tiles):
        span = slice(pair * LANES, (pair + 1) * LANES)
        x = x_ref[:, span]
        parts = []
        mixed = []
        for h in (2 * pair, 2 * pair + 1):
            differ = column(h) - cumulative[h : h + 1, :]
            decay = jnp.exp(jnp.where(lower, differ, FAR_BELOW))
            weights = (products * decay * dt[h : h + 1, :]).astype(jnp.bfloat16)
            parts.append(jnp.dot(weights, x, preferred_element_type=jnp.float32))
            mixed.append((column(2 * heads + h) * b_wide).astype(jnp.bfloat16))
        gain = jnp.where(first_head, skip_ref[2 * pair], skip_ref[2 * pair + 1])
        raw[:, span] = jnp.where(first_head, parts[0], parts[1]) + gain * x.astype(
            jnp.float32
        )
        reach[:, span] = jnp.where(
            first_head, column(heads + 2 * pair), column(heads + 2 * pair + 1)
        )
        z = z_ref[:, span].astype(jnp.float32)
        silu[:, span] = z / (1.0 + jnp.exp(-z))
        both = lax.dot_general(
            x,
            jnp.concatenate(mixed, axis=1),
            (((0,), (0,)), ((), ())),
            preferred_element_type=jnp.float32,
        )
        top = pair * LANES
        fresh[top : top + HEAD_DIM] = both[:HEAD_DIM, :LANES]
        fresh[top + HEAD_DIM : top + LANES] = both[HEAD_DIM:, LANES:]

    live = row_id < length
    scores = functools.partial(
        lax.dot_general,
        dimension_numbers=(((1,), (1,)), ((), ())),
        preferred_element_type=jnp.float32,
    )

    def attend(head, keys, values, seen):
        old = jnp.where(seen, scores(q_ref[:, head * LANES : (head + 1) * LANES], keys), FAR_BELOW)
        top = jnp.max(old, axis=1, keepdims=True)
        old = jnp.exp((old - top) * SCORE_SCALE)
        weight = jnp.sum(old, axis=1, keepdims=True)
        out = jnp.dot(old.astype(jnp.bfloat16), values, preferred_element_type=jnp.float32)
        wide = (tokens, LANES)
        return jnp.broadcast_to(top, wide), jnp.broadcast_to(weight, wide), out

    def merge(one, two):
        top = jnp.maximum(one[0], two[0])
        left = jnp.exp((one[0] - top) * SCORE_SCALE)
        right = jnp.exp((two[0] - top) * SCORE_SCALE)
        return top, one[1] * left + two[1] * right, one[2] * left + two[2] * right

    keys_new = new_ref[:, :LANES]
    values_new = new_ref[:, LANES:]
    for head in range(tiles):
        span = slice(head * LANES, (head + 1) * LANES)
        best[:, span], total_weight[:, span], partial_out[:, span] = attend(
            head, keys_new, values_new, lower
        )

    arrived(state_mid, 0, others)
    collect(state_mid, state_fwd, state_in, 2, 2, in_turn)
    arrived(kv_mid, 1, others)

    @pl.when(side == 0)
    def _():
        collect(kv_mid, kv_fwd, kv_in, 3, 3, in_turn)

    @pl.when(side == 1)
    def _():
        collect(kv_mid, kv_fwd, kv_in, 3, 4, in_turn)

    arrived(state_in, 2, others)
    state = state_in[...].reshape(x_ref.shape[1], LANES)
    total = jnp.zeros((tokens, LANES), jnp.float32)
    for pair in range(tiles):
        span = slice(pair * LANES, (pair + 1) * LANES)
        carried = lax.dot_general(
            c, state[span], (((1,), (1,)), ((), ())), preferred_element_type=jnp.float32
        )
        gated = (raw[:, span] + reach[:, span] * carried) * silu[:, span]
        raw[:, span] = gated
        total = total + gated * gated
    squares = jnp.sum(jnp.transpose(total), axis=0, keepdims=True)
    square_out[...] = jnp.broadcast_to(squares, square_out.shape)
    square_in[rank] = jnp.broadcast_to(squares, square_out.shape)

    def tell(k, carry):
        peer = lax.rem(rank + k, ranks)
        pltpu.make_async_remote_copy(
            src_ref=square_out,
            dst_ref=square_in.at[rank],
            send_sem=square_send,
            recv_sem=square_recv,
            device_id={"tp": peer},
            device_id_type=MESH,
        ).start()
        return carry

    lax.fori_loop(1, ranks, tell, 0)
    for h in range(heads):
        span = slice(h * HEAD_DIM, (h + 1) * HEAD_DIM)
        new_state_ref[span] = (
            final[h : h + 1, :] * state[span].astype(jnp.float32) + fresh[span]
        ).astype(jnp.bfloat16)

    part = square_in.at[pl.ds(0, ranks - 1)]
    pltpu.make_async_copy(part, part, square_recv).wait()
    mean = jnp.sum(square_in[...], axis=0) / (x_ref.shape[1] * ranks)
    scale = lax.rsqrt(mean + EPSILON)
    scale = jnp.transpose(jnp.broadcast_to(scale[:1], (tokens, tokens)))
    scale = jnp.where(live, scale, 0.0)
    for pair in range(tiles):
        span = slice(pair * LANES, (pair + 1) * LANES)
        mixer_ref[:, span] = (raw[:, span] * scale * gain_ref[:, span]).astype(jnp.bfloat16)


    cached = cached_len_ref[source_ref[me]]
    key_id = lax.broadcasted_iota(jnp.int32, (tokens, half // 2 * PAGE), 1)
    for origin in range(2):

        @pl.when(side == origin)
        def _():
            arrived(kv_in, 3 + origin, half - 1)

        @pl.when(side != origin)
        def _():
            arrived(kv_in, 3 + origin, half)

        first = origin * half
        keys = jnp.concatenate([kv_in[first + 2 * p] for p in range(half // 2)], axis=0)
        values = jnp.concatenate(
            [kv_in[first + 2 * p + 1] for p in range(half // 2)], axis=0
        )
        seen = key_id + first // 2 * PAGE < cached
        for head in range(tiles):
            span = slice(head * LANES, (head + 1) * LANES)
            top, weight, out = merge(
                (best[:, span], total_weight[:, span], partial_out[:, span]),
                attend(head, keys, values, seen),
            )
            if origin == 0:
                best[:, span], total_weight[:, span], partial_out[:, span] = top, weight, out
            else:
                attn_ref[:, span] = jnp.where(live, out / weight, 0.0).astype(jnp.bfloat16)

    sent(state_out, 0)
    sent(kv_out, 1)
    sent(state_fwd, 2)
    sent(kv_fwd, 3)
    part = square_in.at[pl.ds(0, ranks - 1)]
    pltpu.make_async_copy(part, part, square_send).wait()


def on_device(
    instances,
    ranks,
    cached_state,
    kv_pool,
    page_table,
    cached_len,
    source_session,
    turn_len,
    x_inner,
    gate_z,
    b_proj,
    c_proj,
    step_size,
    decay_rate,
    skip_gain,
    norm_gain,
    queries,
    new_kv,
):
    stores, rows, width = cached_state.shape
    piece = (instances, PAGE, LANES)
    tokens, inner = x_inner.shape
    hbm = pl.BlockSpec(memory_space=pltpu.HBM)
    operands = (
        (source_session, pltpu.SMEM),
        (page_table, pltpu.SMEM),
        (cached_state.reshape(stores, instances, PAGE, width), pltpu.VMEM),
        (kv_pool, pltpu.VMEM),
        (turn_len, pltpu.SMEM),
        (decay_rate, pltpu.SMEM),
        (skip_gain, pltpu.SMEM),
        (x_inner, pltpu.VMEM),
        (b_proj, pltpu.VMEM),
        (c_proj, pltpu.VMEM),
        (step_size, pltpu.VMEM),
        (gate_z, pltpu.VMEM),
        (norm_gain.reshape(1, inner), pltpu.VMEM),
        (cached_len, pltpu.SMEM),
        (queries, pltpu.VMEM),
        (new_kv, pltpu.VMEM),
    )
    results = (
        jax.ShapeDtypeStruct((2, tokens, inner), jnp.bfloat16),
        jax.ShapeDtypeStruct((rows, width), jnp.bfloat16),
    )
    token_rows, new_state = pl.pallas_call(
        functools.partial(serve_kernel, instances, ranks),
        out_shape=results,
        in_specs=[hbm] * N_OPERANDS,
        out_specs=(pl.BlockSpec(memory_space=pltpu.VMEM),) * N_OUTPUTS,
        scratch_shapes=[space(array.shape, array.dtype) for array, space in operands]
        + [pltpu.VMEM(piece, jnp.bfloat16)] * 8
        + [
            pltpu.VMEM((8, LANES), jnp.float32),
            pltpu.VMEM((ranks, 8, LANES), jnp.float32),
            pltpu.VMEM((tokens, inner), jnp.float32),
            pltpu.VMEM((tokens, inner), jnp.float32),
            pltpu.VMEM((tokens, inner), jnp.float32),
            pltpu.VMEM((rows, width), jnp.float32),
            pltpu.SemaphoreType.DMA((4,)),
            pltpu.SemaphoreType.DMA((5,)),
            pltpu.SemaphoreType.DMA,
            pltpu.SemaphoreType.DMA,
            pltpu.SemaphoreType.DMA((N_OPERANDS,)),
            pltpu.VMEM((tokens, inner), jnp.float32),
            pltpu.VMEM((tokens, inner), jnp.float32),
            pltpu.VMEM((tokens, inner), jnp.float32),
        ],
        compiler_params=pltpu.CompilerParams(
            collective_id=0, has_side_effects=True, vmem_limit_bytes=48 * 1024 * 1024
        ),
    )(*((array if array.size == 1 else pltpu.with_memory_space_constraint(array, pltpu.HBM)) for array, _ in operands))
    mixer_out, attn_out = token_rows[0], token_rows[1]
    return (mixer_out, attn_out, new_state.reshape(1, rows, width))


def solution(mesh):
    in_specs = (
        P("inst", "tp", None),
        P("inst", None, "tp"),
        P("inst", None),
        P(),
        P(),
        P("inst"),
        P("inst", "tp"),
        P("inst", "tp"),
        P("inst", "tp"),
        P("inst", "tp"),
        P("tp", "inst"),
        P("tp"),
        P("tp"),
        P("tp"),
        P("inst", "tp"),
        P("inst", "tp"),
    )
    out_specs = (P("inst", "tp"), P("inst", "tp"), P("inst", "tp", None))
    body = functools.partial(on_device, mesh.shape["inst"], mesh.shape["tp"])
    return jax.shard_map(
        body, mesh=mesh, in_specs=in_specs, out_specs=out_specs, check_vma=False
    )
```
